32 devices in a mesh: fsdp: 16 (over z, y, core), tensor: 2 (over x).
Axes of the slice: x: 2, y: 2, z: 4, core: 2. Of those that a mesh axis runs over, the one named last changes fastest.
Arguments:
- images: float32 [16, 200, 384], P('fsdp', 'tensor'), may hold values from -6 to 6
- upstream: float32 [16, 200, 384], P('fsdp', 'tensor'), may hold values from -6 to 6
- image_count: int32 [16], P('fsdp'), may hold values from 0 to 1, as said below
- valid_tokens: int32 [16], P('fsdp'), may hold values from 165 to 197, as said below
- qkv_weight: bfloat16 [2, 3, 384, 384], P(None, None, 'fsdp', 'tensor'), may hold values from -0.3125 to 0.3125
- qv_bias: float32 [2, 2, 384], replicated, may hold values from -2 to 2
- out_weight: bfloat16 [2, 384, 384], P(None, 'tensor', 'fsdp'), may hold values from -1.25 to 1.25
- out_bias: float32 [2, 384], replicated, may hold values from -2 to 2
- gain_one: float32 [2, 384], replicated, may hold values from 0.1 to 1.9
- shift_one: float32 [2, 384], replicated, may hold values from -2 to 2
- gain_two: float32 [2, 384], replicated, may hold values from 0.1 to 1.9
- shift_two: float32 [2, 384], replicated, may hold values from -2 to 2
- up_weight: bfloat16 [2, 384, 1536], P(None, 'fsdp', 'tensor'), may hold values from -0.3125 to 0.3125
- up_bias: float32 [2, 1536], replicated, may hold values from -2 to 2
- down_weight: bfloat16 [2, 1536, 384], P(None, 'tensor', 'fsdp'), may hold values from -0.15625 to 0.15625
- down_bias: float32 [2, 384], replicated, may hold values from -2 to 2
Outputs:
- output: float32 [16, 200, 384], P('fsdp', 'tensor')
- grad_images: float32 [16, 200, 384], P('fsdp', 'tensor')
- qkv_grad: float32 [2, 3, 384, 384], P(None, None, 'fsdp', 'tensor')
- qv_bias_grad: float32 [2, 2, 384], replicated
- out_grad: float32 [2, 384, 384], P(None, 'tensor', 'fsdp')
- out_bias_grad: float32 [2, 384], replicated
- gain_one_grad: float32 [2, 384], replicated
- shift_one_grad: float32 [2, 384], replicated
- gain_two_grad: float32 [2, 384], replicated
- shift_two_grad: float32 [2, 384], replicated
- up_grad: float32 [2, 384, 1536], P(None, 'fsdp', 'tensor')
- up_bias_grad: float32 [2, 1536], replicated
- down_grad: float32 [2, 1536, 384], P(None, 'tensor', 'fsdp')
- down_bias_grad: float32 [2, 384], replicated
The draws below stay inside these ranges and needn't reach their ends.
Inputs may be any that keep to these rules, and one draw needn't show every extreme that they name: `image_count`: the live images of an index of fsdp fill its first slots; some index holds 1. `valid_tokens`: some slot has 197 tokens that count.
All inputs are finite; a program needn't handle non-finite values.
Results may differ from the reference program's by a relative error of at most 0.02.
Values may be sent and summed in bfloat16 or wider, within the bound.
A program may use at most 128 MiB of HBM per device.

```python
import jax
import jax.numpy as jnp
from jax import lax

D = 384
H = 6
HD = 64
FF = 1536
LIVE = 197
SEQ = 200
LAYERS = 2
IMG_CAP = 1
SLOTS = 16
N_FSDP = 16


def draw_image_count(key, part):
    key = jax.random.fold_in(key, 11)
    first, second = jax.random.split(key)
    counts = jax.random.randint(first, (N_FSDP,), 0, IMG_CAP + 1)
    chosen = jax.random.randint(second, (), 0, N_FSDP)
    return jnp.where(jnp.arange(N_FSDP) == chosen, IMG_CAP, counts).astype(jnp.int32)


def draw_valid_tokens(key, part):
    key = jax.random.fold_in(key, 23)
    first, second = jax.random.split(key)
    lengths = jax.random.randint(first, (SLOTS,), LIVE - LIVE // 6, LIVE + 1)
    chosen = jax.random.randint(second, (), 0, SLOTS)
    return jnp.where(jnp.arange(SLOTS) == chosen, LIVE, lengths).astype(jnp.int32)


def steps_of(rng, extent, cuts, low, top_value):
    def one(position, blocks):
        draws = jax.random.uniform(jax.random.fold_in(jax.random.fold_in(rng, 6), position), (blocks,), jnp.float32, low / len(cuts), top_value / len(cuts))
        return jnp.repeat(jnp.exp(draws), extent[position] // blocks).reshape((-1,) + (1,) * (len(extent) - position - 1))

    loudness = one(*cuts[0])
    for cut in cuts[1:]:
        loudness = loudness * one(*cut)
    return loudness


def gaussian(key, shape, width, most, shards=(), held_as=jnp.bfloat16):
    values = width * jax.random.normal(key, shape, jnp.float32)
    if shards:
        values = values * steps_of(key, shape, shards, -0.22, 0.18)
    return jnp.clip(values, -most, most).astype(held_as)


def setup_inputs(seed: int = 0) -> dict:
    key_of = jax.random.split(jax.random.key(seed), 17)
    images = gaussian(key_of[0], (SLOTS, SEQ, D), 1.0, 6.0, ((0, 16), (1, 2)), jnp.float32)
    upstream = gaussian(key_of[1], (SLOTS, SEQ, D), 1.0, 6.0, ((0, 16), (1, 2)), jnp.float32)
    image_count = draw_image_count(jax.random.fold_in(key_of[16], 71), 0)
    valid_tokens = draw_valid_tokens(jax.random.fold_in(key_of[16], 71), 0)
    qkv_weight = gaussian(key_of[4], (LAYERS, 3, D, D), D ** -0.5, 0.3125, ((2, 16), (3, 2)))
    qv_bias = gaussian(key_of[5], (LAYERS, 2, D), 0.3, 2.0, (), jnp.float32)
    out_weight = gaussian(key_of[6], (LAYERS, D, D), (D // 16) ** -0.5, 1.25, ((1, 2), (2, 16)))
    out_bias = gaussian(key_of[7], (LAYERS, D), 0.3, 2.0, (), jnp.float32)
    gain_one = jnp.clip(1.0 + 0.18 * jax.random.normal(key_of[8], (LAYERS, D), jnp.float32), 0.1, 1.9)
    shift_one = gaussian(key_of[9], (LAYERS, D), 0.3, 2.0, (), jnp.float32)
    gain_two = jnp.clip(1.0 + 0.18 * jax.random.normal(key_of[10], (LAYERS, D), jnp.float32), 0.1, 1.9)
    shift_two = gaussian(key_of[11], (LAYERS, D), 0.3, 2.0, (), jnp.float32)
    up_weight = gaussian(key_of[12], (LAYERS, D, FF), D ** -0.5, 0.3125, ((1, 16), (2, 2)))
    up_bias = gaussian(key_of[13], (LAYERS, FF), 0.3, 2.0, (), jnp.float32)
    down_weight = gaussian(key_of[14], (LAYERS, FF, D), FF ** -0.5, 0.15625, ((1, 2), (2, 16)))
    down_bias = gaussian(key_of[15], (LAYERS, D), 0.3, 2.0, (), jnp.float32)
    return dict(images=images, upstream=upstream, image_count=image_count, valid_tokens=valid_tokens, qkv_weight=qkv_weight, qv_bias=qv_bias, out_weight=out_weight, out_bias=out_bias, gain_one=gain_one, shift_one=shift_one, gain_two=gain_two, shift_two=shift_two, up_weight=up_weight, up_bias=up_bias, down_weight=down_weight, down_bias=down_bias)


@jax.custom_vjp
def low(v):
    return lax.optimization_barrier(v.astype(jnp.bfloat16)).astype(jnp.float32)

@jax.custom_vjp
def low_back(v):
    return v

def low_keep(v):
    return (low(v), None)

def low_pass(kept, grad):
    return (grad,)

def back_keep(v):
    return (v, None)

def back_low(kept, grad):
    return (low(grad),)
low.defvjp(low_keep, low_pass)
low_back.defvjp(back_keep, back_low)
epsilon = 1e-06
highest = lax.Precision.HIGHEST

def norm_rows(hidden, gain, shift):
    centre = hidden - lax.optimization_barrier(jnp.mean(hidden, axis=-1, keepdims=True))
    spread = lax.optimization_barrier(jnp.mean(centre * centre, axis=-1, keepdims=True))
    return centre * lax.rsqrt(spread + epsilon) * gain + shift

def encoder_layer(hidden, qkv_weight, qv_bias, out_weight, out_bias, gain_one, shift_one, gain_two, shift_two, up_weight, up_bias, down_weight, down_bias, key_ok):
    image_total, length, model_width = hidden.shape
    normed = low(norm_rows(hidden, gain_one, shift_one))
    project = jnp.einsum('gtd,cde->cgte', normed, qkv_weight, precision=highest)
    queries = low_back(low(project[0] + qv_bias[0])).reshape(image_total, length, H, HD)
    key_rows = low_back(low(project[1])).reshape(image_total, length, H, HD)
    values = low_back(low(project[2] + qv_bias[1])).reshape(image_total, length, H, HD)
    scores = low_back(jnp.einsum('gqhd,gkhd->ghqk', queries, key_rows, precision=highest) * HD ** (-0.5))
    scores = jnp.where(key_ok[:, None, None, :], scores, -1e+30)
    highest_score = lax.optimization_barrier(jnp.max(scores, axis=-1, keepdims=True))
    exponent = jnp.exp(scores - highest_score)
    portions = low(exponent / lax.optimization_barrier(jnp.sum(exponent, axis=-1, keepdims=True)))
    mixed = jnp.einsum('ghqk,gkhd->gqhd', portions, values, precision=highest).reshape(image_total, length, model_width)
    mixed = low_back(low(mixed))
    branch = low_back(jnp.einsum('gte,ed->gtd', mixed, out_weight, precision=highest) + out_bias)
    middle = hidden + branch
    normed_two = low(norm_rows(middle, gain_two, shift_two))
    up_value = low_back(jnp.einsum('gtd,df->gtf', normed_two, up_weight, precision=highest) + up_bias)
    activated = low(jax.nn.gelu(up_value, approximate=False))
    branch_two = low_back(jnp.einsum('gtf,fd->gtd', activated, down_weight, precision=highest) + down_bias)
    return middle + branch_two

def forward(inputs, qkv_weight, qv_bias, out_weight, out_bias, gain_one, shift_one, gain_two, shift_two, up_weight, up_bias, down_weight, down_bias, key_ok, row_ok):
    hidden = inputs
    for layer_index in range(LAYERS):
        hidden = encoder_layer(hidden, qkv_weight[layer_index], qv_bias[layer_index], out_weight[layer_index], out_bias[layer_index], gain_one[layer_index], shift_one[layer_index], gain_two[layer_index], shift_two[layer_index], up_weight[layer_index], up_bias[layer_index], down_weight[layer_index], down_bias[layer_index], key_ok)
    return hidden * row_ok[:, :, None]

def reference(images, upstream, image_count, valid_tokens, qkv_weight, qv_bias, out_weight, out_bias, gain_one, shift_one, gain_two, shift_two, up_weight, up_bias, down_weight, down_bias):
    weights_full = (qkv_weight.astype(jnp.float32), qv_bias.astype(jnp.float32), out_weight.astype(jnp.float32), out_bias.astype(jnp.float32), gain_one.astype(jnp.float32), shift_one.astype(jnp.float32), gain_two.astype(jnp.float32), shift_two.astype(jnp.float32), up_weight.astype(jnp.float32), up_bias.astype(jnp.float32), down_weight.astype(jnp.float32), down_bias.astype(jnp.float32))
    positions = jnp.arange(SEQ, dtype=jnp.int32)
    slots_live = jnp.arange(IMG_CAP, dtype=jnp.int32)[None, :] < image_count[:, None]
    valid_groups = valid_tokens.reshape(N_FSDP, IMG_CAP)
    input_groups = images.reshape(N_FSDP, IMG_CAP, SEQ, D).astype(jnp.float32)
    grad_groups = upstream.reshape(N_FSDP, IMG_CAP, SEQ, D).astype(jnp.float32)

    def group_step(totals, inputs):
        block, grad_out, slot_live, valid = inputs
        key_ok = positions[None, :] < valid[:, None]
        row_ok = jnp.where(key_ok & slot_live[:, None], 1.0, 0.0).astype(jnp.float32)

        def closed(block_in, *weights):
            return forward(block_in, *weights, key_ok, row_ok)
        result, back = jax.vjp(closed, block, *weights_full)
        grads = back(grad_out)
        totals = tuple((total + grad for total, grad in zip(totals, grads[1:])))
        return (totals, (result, grads[0]))
    zeros = tuple((jnp.zeros_like(weight) for weight in weights_full))
    totals, (results, grad_inputs) = lax.scan(group_step, zeros, (input_groups, grad_groups, slots_live, valid_groups))
    return (results.reshape(SLOTS, SEQ, D), grad_inputs.reshape(SLOTS, SEQ, D), totals[0], totals[1], totals[2], totals[3], totals[4], totals[5], totals[6], totals[7], totals[8], totals[9], totals[10], totals[11])
```

```python
from functools import partial

import jax
import jax.numpy as jnp
from jax import lax
from jax.experimental import pallas as pl
from jax.experimental.pallas import tpu as pltpu
from jax.sharding import PartitionSpec as P

D = 384
HD = 64
FF = 1536


epsilon = 1e-06


def norm_rows(hidden, gain, shift):
    centre = hidden - jnp.mean(hidden, axis=-1, keepdims=True)
    spread = jnp.mean(centre * centre, axis=-1, keepdims=True)
    return centre * lax.rsqrt(spread + epsilon) * gain + shift


def take_half(vector, width_here, index):
    return lax.dynamic_slice_in_dim(vector, index * width_here, width_here, vector.ndim - 1)


def widen_half(vector, index, total):
    empty = jnp.zeros(vector.shape[:-1] + (total,), jnp.float32)
    return lax.dynamic_update_slice_in_dim(empty, vector, index * vector.shape[-1], vector.ndim - 1)


def head_split(array):
    slot_count, length, head_width = array.shape
    return array.reshape(slot_count, length, head_width // HD, HD)


def masked_scores(queries, key_rows, key_ok):
    scores = jnp.einsum(
        "sqhd,skhd->shqk",
        head_split(queries),
        head_split(key_rows),
        preferred_element_type=jnp.float32,
    ) * HD ** (-0.5)
    return jnp.where(key_ok[:, None, None, :], scores, -1e30)


def attend(queries, key_rows, values, key_ok):
    scores = masked_scores(queries, key_rows, key_ok)
    highest_score = jnp.max(scores, axis=-1, keepdims=True)
    log_total = highest_score + jnp.log(
        jnp.sum(jnp.exp(scores - highest_score), axis=-1, keepdims=True)
    )
    portions = jnp.exp(scores - log_total).astype(jnp.bfloat16)
    mixed = jnp.einsum(
        "shqk,skhd->sqhd", portions, head_split(values), preferred_element_type=jnp.float32
    )
    return (log_total, mixed.reshape(queries.shape).astype(jnp.bfloat16))


def attend_back(queries, key_rows, values, log_total, grad_mixed, key_ok):
    portions = jnp.exp(masked_scores(queries, key_rows, key_ok) - log_total)
    grad_heads = head_split(grad_mixed)
    grad_portions = jnp.einsum(
        "sqhd,skhd->shqk", grad_heads, head_split(values), preferred_element_type=jnp.float32
    )
    grad_values = jnp.einsum(
        "shqk,sqhd->skhd",
        portions.astype(jnp.bfloat16),
        grad_heads,
        preferred_element_type=jnp.float32,
    )
    inner_sum = jnp.sum(portions * grad_portions, axis=-1, keepdims=True)
    grad_scores = (portions * (grad_portions - inner_sum)).astype(jnp.bfloat16)
    grad_queries = jnp.einsum(
        "shqk,skhd->sqhd", grad_scores, head_split(key_rows), preferred_element_type=jnp.float32
    ) * HD ** (-0.5)
    grad_keys = jnp.einsum(
        "shqk,sqhd->skhd", grad_scores, head_split(queries), preferred_element_type=jnp.float32
    ) * HD ** (-0.5)
    full_shape = queries.shape
    return (
        grad_queries.reshape(full_shape).astype(jnp.bfloat16),
        grad_keys.reshape(full_shape).astype(jnp.bfloat16),
        grad_values.reshape(full_shape).astype(jnp.bfloat16),
    )


def fetch_weights(qkv_part, out_part, up_part, down_part):
    return (
        lax.all_gather(qkv_part, "fsdp", axis=1, tiled=True),
        lax.all_gather(out_part, "fsdp", axis=1, tiled=True),
        lax.all_gather(up_part, "fsdp", axis=0, tiled=True),
        lax.all_gather(down_part, "fsdp", axis=1, tiled=True),
    )


def share_tokens(value):
    return lax.all_gather(value, "tensor", axis=1, tiled=True)


def sum_branch(value):
    return lax.psum_scatter(
        value.astype(jnp.bfloat16), "tensor", scatter_dimension=1, tiled=True
    ).astype(jnp.float32)


def gather_grads(value):
    return lax.all_gather(value, "tensor", axis=1, tiled=True)


def sum_inputs(value):
    return lax.psum_scatter(
        value.astype(jnp.bfloat16), "tensor", scatter_dimension=1, tiled=True
    ).astype(jnp.float32)


def local(
    images,
    upstream,
    image_count,
    valid_tokens,
    qkv_weight,
    qv_bias,
    out_weight,
    out_bias,
    gain_one,
    shift_one,
    gain_two,
    shift_two,
    up_weight,
    up_bias,
    down_weight,
    down_bias,
):
    slot_count, half_length, model_width = images.shape
    tensor_size = lax.axis_size("tensor")
    tensor_rank = lax.axis_index("tensor")
    length = half_length * tensor_size
    head_width = qkv_weight.shape[3]
    hidden_width = up_weight.shape[2]
    layer_count = qkv_weight.shape[0]
    key_ok = jnp.arange(length, dtype=jnp.int32)[None, :] < valid_tokens[:, None]
    slot_live = jnp.arange(slot_count, dtype=jnp.int32) < image_count[0]
    own_rows = tensor_rank * half_length + jnp.arange(half_length, dtype=jnp.int32)
    row_ok = jnp.where(
        (own_rows[None, :] < valid_tokens[:, None]) & slot_live[:, None], 1.0, 0.0
    ).astype(jnp.float32)
    stored = []
    hidden = images
    for layer_index in range(layer_count):
        fetched = fetch_weights(
            qkv_weight[layer_index],
            out_weight[layer_index],
            up_weight[layer_index],
            down_weight[layer_index],
        )
        qkv_full, out_full, up_full, down_full = fetched
        bias_pair = take_half(qv_bias[layer_index], head_width, tensor_rank)
        normed = norm_rows(hidden, gain_one[layer_index], shift_one[layer_index]).astype(
            jnp.bfloat16
        )
        shared = share_tokens(normed)
        project = jnp.einsum("std,cde->cste", shared, qkv_full, preferred_element_type=jnp.float32)
        queries = (project[0] + bias_pair[0]).astype(jnp.bfloat16)
        key_rows = project[1].astype(jnp.bfloat16)
        values = (project[2] + bias_pair[1]).astype(jnp.bfloat16)
        log_total, mixed = attend(queries, key_rows, values, key_ok)
        branch = sum_branch(
            jnp.einsum("ste,ed->std", mixed, out_full, preferred_element_type=jnp.float32)
        )
        middle = hidden + (branch + out_bias[layer_index])
        normed_two = norm_rows(middle, gain_two[layer_index], shift_two[layer_index]).astype(
            jnp.bfloat16
        )
        shared_two = share_tokens(normed_two)
        up_value = jnp.einsum(
            "std,df->stf", shared_two, up_full, preferred_element_type=jnp.float32
        ) + take_half(up_bias[layer_index], hidden_width, tensor_rank)
        activated = jax.nn.gelu(up_value, approximate=False).astype(jnp.bfloat16)
        branch_two = sum_branch(
            jnp.einsum("stf,fd->std", activated, down_full, preferred_element_type=jnp.float32)
        )
        stored.append(
            (
                hidden,
                shared,
                queries,
                key_rows,
                values,
                log_total,
                mixed,
                middle,
                shared_two,
                up_value,
                activated,
                fetched,
            )
        )
        hidden = middle + (branch_two + down_bias[layer_index])
    output = hidden * row_ok[:, :, None]
    grad_hidden = upstream * row_ok[:, :, None]
    large_grads = [None] * layer_count
    small_grads = [None] * layer_count
    for layer_index in reversed(range(layer_count)):
        (
            hidden_in,
            shared,
            queries,
            key_rows,
            values,
            log_total,
            mixed,
            middle,
            shared_two,
            up_value,
            activated,
            fetched,
        ) = stored[layer_index]
        qkv_full, out_full, up_full, down_full = (
            lax.all_gather(qkv_weight[layer_index], "fsdp", axis=1, tiled=True),
            lax.all_gather(out_weight[layer_index], "fsdp", axis=1, tiled=True),
            lax.all_gather(up_weight[layer_index], "fsdp", axis=0, tiled=True),
            lax.all_gather(down_weight[layer_index], "fsdp", axis=1, tiled=True),
        )
        grad_branch = grad_hidden.astype(jnp.bfloat16)
        down_bias_grad = jnp.sum(grad_branch.astype(jnp.float32), axis=(0, 1))
        grad_rows = gather_grads(grad_branch)
        down_grad = jnp.einsum(
            "stf,std->fd", activated, grad_rows, preferred_element_type=jnp.float32
        )
        grad_activated = jnp.einsum(
            "std,fd->stf", grad_rows, down_full, preferred_element_type=jnp.float32
        )
        gelu_back = jax.vjp(partial(jax.nn.gelu, approximate=False), up_value)[1]
        grad_up = gelu_back(grad_activated)[0].astype(jnp.bfloat16)
        up_bias_grad = widen_half(
            jnp.sum(grad_up.astype(jnp.float32), axis=(0, 1)), tensor_rank, FF
        )
        up_grad = jnp.einsum("std,stf->df", shared_two, grad_up, preferred_element_type=jnp.float32)
        grad_normed_two = sum_inputs(
            jnp.einsum("stf,df->std", grad_up, up_full, preferred_element_type=jnp.float32)
        )
        norm_back = jax.vjp(norm_rows, middle, gain_two[layer_index], shift_two[layer_index])[1]
        grad_from_norm, gain_two_grad, shift_two_grad = norm_back(grad_normed_two)
        grad_middle = grad_hidden + grad_from_norm
        grad_branch = grad_middle.astype(jnp.bfloat16)
        out_bias_grad = jnp.sum(grad_branch.astype(jnp.float32), axis=(0, 1))
        grad_rows = gather_grads(grad_branch)
        out_grad = jnp.einsum("ste,std->ed", mixed, grad_rows, preferred_element_type=jnp.float32)
        grad_mixed = jnp.einsum(
            "std,ed->ste", grad_rows, out_full, preferred_element_type=jnp.float32
        ).astype(jnp.bfloat16)
        grad_queries, grad_keys, grad_values = attend_back(
            queries, key_rows, values, log_total, grad_mixed, key_ok
        )
        grad_project = jnp.stack([grad_queries, grad_keys, grad_values])
        qkv_grad = jnp.einsum(
            "std,cste->cde", shared, grad_project, preferred_element_type=jnp.float32
        )
        qv_sums = jnp.stack(
            [
                jnp.sum(grad_queries.astype(jnp.float32), axis=(0, 1)),
                jnp.sum(grad_values.astype(jnp.float32), axis=(0, 1)),
            ]
        )
        qv_bias_grad = widen_half(qv_sums, tensor_rank, D)
        grad_normed = sum_inputs(
            jnp.einsum("cste,cde->std", grad_project, qkv_full, preferred_element_type=jnp.float32)
        )
        norm_back = jax.vjp(norm_rows, hidden_in, gain_one[layer_index], shift_one[layer_index])[1]
        grad_input, gain_one_grad, shift_one_grad = norm_back(grad_normed)
        grad_hidden = grad_middle + grad_input
        large_grads[layer_index] = (
            lax.psum_scatter(qkv_grad, "fsdp", scatter_dimension=1, tiled=True),
            lax.psum_scatter(out_grad, "fsdp", scatter_dimension=1, tiled=True),
            lax.psum_scatter(up_grad, "fsdp", scatter_dimension=0, tiled=True),
            lax.psum_scatter(down_grad, "fsdp", scatter_dimension=1, tiled=True),
        )
        small_grads[layer_index] = (
            qv_bias_grad,
            out_bias_grad,
            gain_one_grad,
            shift_one_grad,
            gain_two_grad,
            shift_two_grad,
            up_bias_grad,
            down_bias_grad,
        )
    stacked = tuple(
        (
            jnp.stack([large_grads[layer_index][member] for layer_index in range(layer_count)])
            for member in range(4)
        )
    )
    small_stacked = tuple(
        (
            jnp.stack([small_grads[layer_index][member] for layer_index in range(layer_count)])
            for member in range(8)
        )
    )
    summed = lax.psum(
        (
            small_stacked[0],
            small_stacked[1],
            small_stacked[2],
            small_stacked[3],
            small_stacked[4],
            small_stacked[5],
            small_stacked[6],
            small_stacked[7],
        ),
        ("fsdp", "tensor"),
    )
    return (
        output,
        grad_hidden,
        stacked[0],
        summed[0],
        stacked[1],
        summed[1],
        summed[2],
        summed[3],
        summed[4],
        summed[5],
        stacked[2],
        summed[6],
        stacked[3],
        summed[7],
    )


BF = jnp.bfloat16
F32 = jnp.float32
HALF = 112
ROWS = 2 * HALF
WIDE = 1280
FFN = pl.ds(0, 768)
ATT = pl.ds(768, 512)
PARTS = (FFN, ATT)
COPIES = 82


def dot(a, b, ca, cb):
    return lax.dot_general(a, b, (((ca,), (cb,)), ((), ())), preferred_element_type=F32)


def row_stats(x):
    centre = x - jnp.mean(x, axis=-1, keepdims=True)
    r = lax.rsqrt(jnp.mean(centre * centre, axis=-1, keepdims=True) + epsilon)
    return centre * r, r


def norm_grad(e, xhat, r, gain):
    gy = e * gain
    return r * (
        gy
        - jnp.mean(gy, axis=-1, keepdims=True)
        - xhat * jnp.mean(gy * xhat, axis=-1, keepdims=True)
    )


def col_sum(x):
    return jnp.sum(x, axis=0, keepdims=True)


def fused_kernel(
    count_ref, valid_ref, img_ref, ups_ref, pack_ref, vec_ref, qvb_ref, upb_ref,
    out_ref, gimg_ref, gw_ref, small_ref,
    w_ref, pr_ref, hid_ref, mid_ref, g_ref, n1_ref, n2_ref, q_ref, k_ref, v_ref, p_ref,
    mix_ref, act_ref, dg_ref, xs_ref, xr_ref, gs_ref, r1_ref, s1_ref, r2_ref, s2_ref,
    r3_ref, s3_ref, sm_ref, smr_ref, smz_ref, send_sem, recv_sem,
):
    f = lax.axis_index("fsdp")
    x = lax.axis_index("tensor")
    c = lax.rem(f, 2)
    y = lax.rem(f // 2, 2)
    z = f // 4

    def at(zz, yy, cc):
        return {"fsdp": zz * 4 + yy * 2 + cc}

    core_peer = at(z, y, 1 - c)
    y_peer = at(z, 1 - y, c)
    x_peer = {"tensor": 1 - x}
    z_next = [lax.rem(z + d, 4) for d in range(4)]
    z_from = [lax.rem(z + 4 - d, 4) for d in range(4)]

    barrier = pltpu.get_barrier_semaphore()
    greeted = [core_peer, y_peer, x_peer] + [at(z_next[d], y, c) for d in (1, 2, 3)]
    for peer in greeted:
        pl.semaphore_signal(barrier, inc=1, device_id=peer, device_id_type=pl.DeviceIdType.MESH)
    pl.semaphore_wait(barrier, len(greeted))

    started = []

    def send(src, dst, peer):
        i = len(started)
        copy = pltpu.make_async_remote_copy(
            src_ref=src, dst_ref=dst, send_sem=send_sem.at[i], recv_sem=recv_sem.at[i],
            device_id=peer, device_id_type=pl.DeviceIdType.MESH,
        )
        copy.start()
        started.append(copy)
        return copy

    pack_copies = [send(pack_ref.at[l, 1 - c], pr_ref.at[l], core_peer) for l in range(2)]

    own_row = lax.broadcasted_iota(jnp.int32, (HALF, 1), 0)
    valid = valid_ref[0]
    own_ok = (own_row < 100) & (x * 100 + own_row < valid) & (count_ref[0] > 0)
    row_ok = jnp.where(own_ok, 1.0, 0.0).astype(F32)
    hid_ref[0, 96:HALF] = jnp.zeros((HALF - 96, 384), F32)
    hid_ref[0, 0:100] = img_ref[...]
    img_copy = send(hid_ref.at[0, 0:HALF], hid_ref.at[0, HALF:ROWS], x_peer)

    z_copies, y_copies, c_copies = {}, {}, {}
    for l in range(2):
        pack_copies[l].wait_recv()
        mine = pack_ref[l, c].astype(F32)[:24]
        theirs = pr_ref[l].astype(F32)[:24]
        first = jnp.broadcast_to(c, mine.shape) == 0
        chunk = jnp.concatenate(
            [jnp.where(first, mine, theirs), jnp.where(first, theirs, mine)], axis=0
        )
        w_ref[l, c, z, y] = chunk.astype(BF)
        for a in (1, 0):
            block = w_ref.at[l, c, z, y, :, PARTS[a]]
            z_copies[l, a] = [send(block, block, at(z_next[d], y, c)) for d in (1, 2, 3)]
            y_copies[l, a] = [send(block, block, y_peer)]

    g_ref[96:HALF] = jnp.zeros((HALF - 96, 384), F32)
    g_ref[0:100] = ups_ref[...]
    g_ref[0:HALF] = g_ref[0:HALF] * row_ok
    ups_copy = send(g_ref.at[0:HALF], g_ref.at[HALF:ROWS], x_peer)

    def gather_y(l, a):
        for d in (1, 2, 3):
            z_copies[l, a][d - 1].wait_recv()
            block = w_ref.at[l, c, z_from[d], y, :, PARTS[a]]
            y_copies[l, a].append(send(block, block, y_peer))

    def gather_core(l, a):
        for copy in y_copies[l, a]:
            copy.wait_recv()
        block = w_ref.at[l, c, :, :, :, PARTS[a]]
        c_copies[l, a] = send(block, block, core_peer)

    def gather_end(l, a):
        c_copies[l, a].wait_recv()

    def x_start(i, value):
        xs_ref[i] = value.astype(BF)
        return [
            send(xs_ref.at[i, HALF:ROWS], xr_ref.at[i, 0:HALF], x_peer),
            send(xs_ref.at[i, 0:HALF], xr_ref.at[i, HALF:ROWS], x_peer),
        ]

    def x_end(i, copies):
        for copy in copies:
            copy.wait_recv()
        return xs_ref[i].astype(F32) + xr_ref[i].astype(F32)

    def weight(l, half, start, size):
        return w_ref[l, half, :, :, :, pl.ds(start, size)].reshape(384, size)

    def vec(l, i):
        return vec_ref[l, i : i + 1]

    lane = lax.broadcasted_iota(jnp.int32, (ROWS, 256), 1)
    head_mask = [
        jnp.where((lane >= HD * h) & (lane < HD * h + HD), 1.0, 0.0).astype(F32).astype(BF)
        for h in range(3)
    ]
    key = lax.broadcasted_iota(jnp.int32, (ROWS, ROWS), 1)
    in_half = jnp.where(key < HALF, key, key - HALF)
    token = in_half + 100 * jnp.where(key < HALF, x, 1 - x)
    key_ok = (in_half < 100) & (token < valid)

    def attention(l):
        xhat, r = row_stats(hid_ref[l])
        n1 = (xhat * vec(l, 1) + vec(l, 2)).astype(BF)
        n1_ref[l] = n1
        yield
        q = (dot(n1, weight(l, 0, 1024, 256), 1, 0) + qvb_ref[l, 0:1]).astype(BF)
        k = dot(n1, weight(l, 1, 768, 256), 1, 0).astype(BF)
        v = (dot(n1, weight(l, 1, 1024, 256), 1, 0) + qvb_ref[l, 1:2]).astype(BF)
        q_ref[l], k_ref[l], v_ref[l] = q, k, v
        mixed = jnp.zeros((ROWS, 256), F32)
        for h in range(3):
            scores = jnp.where(key_ok, dot(q * head_mask[h], k, 1, 1) * HD ** (-0.5), -1e30)
            e = jnp.exp(scores - jnp.max(scores, axis=-1, keepdims=True))
            p = e / jnp.sum(e, axis=-1, keepdims=True)
            p_ref[l, h] = p
            mixed = mixed + dot(p.astype(BF), v * head_mask[h], 1, 0)
        mix_ref[l] = mixed.astype(BF)
        copies = x_start(2 * l, dot(mix_ref[l], weight(l, 0, 768, 256), 1, 1))
        yield
        branch = x_end(2 * l, copies)
        mid_ref[l] = hid_ref[l] + (branch + vec(l, 0))

    def feed(l):
        xhat, r = row_stats(mid_ref[l])
        n2 = (xhat * vec(l, 3) + vec(l, 4)).astype(BF)
        n2_ref[l] = n2
        yield
        up = dot(n2, weight(l, 0, 0, 768), 1, 0) + upb_ref[l]
        phi = 0.5 * (1.0 + lax.erf(up * (0.5**0.5)))
        act_ref[l] = (up * phi).astype(BF)
        dg_ref[l] = phi + up * (jnp.exp(-0.5 * up * up) * 0.3989422804014327)
        copies = x_start(2 * l + 1, dot(act_ref[l], weight(l, 1, 0, 768), 1, 1))
        yield
        branch = x_end(2 * l + 1, copies)
        hid_ref[l + 1] = mid_ref[l] + (branch + vec(l, 5))

    gather_y(0, 1)
    gather_y(0, 0)
    img_copy.wait_recv()
    step = attention(0)
    next(step)
    gather_core(0, 1)
    gather_end(0, 1)
    next(step)
    gather_core(0, 0)
    gather_y(1, 1)
    next(step, None)
    step = feed(0)
    next(step)
    gather_end(0, 0)
    next(step)
    gather_core(1, 1)
    gather_y(1, 0)
    next(step, None)
    step = attention(1)
    next(step)
    gather_end(1, 1)
    next(step)
    gather_core(1, 0)
    next(step, None)
    step = feed(1)
    next(step)
    gather_end(1, 0)
    next(step)
    next(step, None)
    out_ref[...] = (hid_ref[2, 0:HALF] * row_ok)[0:100]
    ups_copy.wait()

    unit = {}

    def reduce_core(l, a):
        part = PARTS[a]
        unit[l, a] = [
            send(gs_ref.at[l, 1 - c, :, :, :, part], r1_ref.at[l, :, :, :, part], core_peer)
        ]

    def reduce_y(l, a):
        part = PARTS[a]
        unit[l, a][0].wait_recv()
        total = gs_ref[l, c, :, :, :, part].astype(F32) + r1_ref[l, :, :, :, part].astype(F32)
        s1_ref[l, :, :, :, part] = total.astype(BF)
        unit[l, a] = [send(s1_ref.at[l, :, 1 - y, :, part], r2_ref.at[l, :, :, part], y_peer)]

    def reduce_z(l, a):
        part = PARTS[a]
        unit[l, a][0].wait_recv()
        total = s1_ref[l, :, y, :, part].astype(F32) + r2_ref[l, :, :, part].astype(F32)
        s2_ref[l, :, :, part] = total.astype(BF)
        unit[l, a] = [
            send(
                s2_ref.at[l, z_next[d], :, part], r3_ref.at[l, d - 1, :, part],
                at(z_next[d], y, c),
            )
            for d in (1, 2, 3)
        ]

    def reduce_last(l, a):
        part = PARTS[a]
        for copy in unit[l, a]:
            copy.wait_recv()
        total = s2_ref[l, z, :, part].astype(F32)
        for d in range(3):
            total = total + r3_ref[l, d, :, part].astype(F32)
        s3_ref[l, :, part] = total
        other = pl.ds(pl.multiple_of(24 * (1 - c), 8), 24)
        own = pl.ds(pl.multiple_of(24 * c, 8), 24)
        unit[l, a] = [send(s3_ref.at[l, other, part], gw_ref.at[l, c, :, part], core_peer)]
        gw_ref[l, c, :, part] = s3_ref[l, own, part]

    def keep(l, half, start, value):
        size = value.shape[1]
        gs_ref[l, half, :, :, :, pl.ds(start, size)] = value.astype(BF).reshape(4, 2, 48, size)

    def feed_back(l):
        g = g_ref[...]
        gb = g.astype(BF)
        ga = dot(gb, weight(l, 1, 0, 768), 1, 0)
        gu = (ga * dg_ref[l]).astype(BF)
        copies = x_start(6 - 2 * l, dot(gu, weight(l, 0, 0, 768), 1, 1))
        keep(l, 1, 0, dot(gb, act_ref[l], 0, 0))
        keep(l, 0, 0, dot(n2_ref[l], gu, 0, 0))
        reduce_core(l, 0)
        yield
        sm_ref[0, 8 * l : 8 * l + 1, :] = col_sum(gu.astype(F32))
        sm_ref[0, 8 * l + 4 : 8 * l + 5, 384:768] = col_sum(gb.astype(F32))
        xhat, r = row_stats(mid_ref[l])
        e = x_end(6 - 2 * l, copies)
        sm_ref[0, 8 * l + 3 : 8 * l + 4, 384:768] = col_sum(e * xhat)
        sm_ref[0, 8 * l + 4 : 8 * l + 5, 0:384] = col_sum(e)
        g_ref[...] = g + norm_grad(e, xhat, r, vec(l, 3))

    def attention_back(l):
        g = g_ref[...]
        gm = g.astype(BF)
        q, k, v = q_ref[l], k_ref[l], v_ref[l]
        gmix = dot(gm, weight(l, 0, 768, 256), 1, 0).astype(BF)
        gq = jnp.zeros((ROWS, 256), F32)
        gk, gv = gq, gq
        for h in range(3):
            p = p_ref[l, h]
            gmh = gmix * head_mask[h]
            dp = dot(gmh, v, 1, 1)
            gv = gv + dot(p.astype(BF), gmh, 0, 0)
            ds = (p * (dp - jnp.sum(p * dp, axis=-1, keepdims=True))).astype(BF)
            gq = gq + dot(ds, k * head_mask[h], 1, 0)
            gk = gk + dot(ds, q * head_mask[h], 0, 0)
        gq = (gq * HD ** (-0.5)).astype(BF)
        gk = (gk * HD ** (-0.5)).astype(BF)
        gv = gv.astype(BF)
        copies = x_start(
            7 - 2 * l,
            dot(gq, weight(l, 0, 1024, 256), 1, 1)
            + dot(gk, weight(l, 1, 768, 256), 1, 1)
            + dot(gv, weight(l, 1, 1024, 256), 1, 1),
        )
        n1 = n1_ref[l]
        keep(l, 0, 768, dot(gm, mix_ref[l], 0, 0))
        keep(l, 0, 1024, dot(n1, gq, 0, 0))
        keep(l, 1, 768, dot(n1, gk, 0, 0))
        keep(l, 1, 1024, dot(n1, gv, 0, 0))
        reduce_core(l, 1)
        yield
        sm_ref[0, 8 * l + 1 : 8 * l + 2, 0:256] = col_sum(gq.astype(F32))
        sm_ref[0, 8 * l + 1 : 8 * l + 2, 256:512] = col_sum(gv.astype(F32))
        sm_ref[0, 8 * l + 2 : 8 * l + 3, 0:384] = col_sum(gm.astype(F32))
        xhat, r = row_stats(hid_ref[l])
        e = x_end(7 - 2 * l, copies)
        sm_ref[0, 8 * l + 2 : 8 * l + 3, 384:768] = col_sum(e * xhat)
        sm_ref[0, 8 * l + 3 : 8 * l + 4, 0:384] = col_sum(e)
        g_ref[...] = g + norm_grad(e, xhat, r, vec(l, 1))

    sm_ref[0] = jnp.zeros((16, 768), F32)
    step = feed_back(1)
    next(step)
    next(step, None)
    step = attention_back(1)
    next(step)
    reduce_y(1, 0)
    next(step, None)
    step = feed_back(0)
    next(step)
    reduce_z(1, 0)
    reduce_y(1, 1)
    next(step, None)
    step = attention_back(0)
    next(step)
    reduce_y(0, 0)
    reduce_z(1, 1)
    reduce_last(1, 0)
    next(step, None)

    small = send(sm_ref.at[0], smr_ref.at[0], core_peer)
    reduce_y(0, 1)
    gimg_ref[...] = g_ref[0:HALF][0:100]
    small.wait_recv()
    sm_ref[1] = sm_ref[0] + smr_ref[0]
    small = send(sm_ref.at[1], smr_ref.at[1], y_peer)
    reduce_z(0, 0)
    reduce_last(1, 1)
    small.wait_recv()
    smz_ref[z] = sm_ref[1] + smr_ref[1]
    smalls = [send(smz_ref.at[z], smz_ref.at[z], at(z_next[d], y, c)) for d in (1, 2, 3)]
    reduce_z(0, 1)
    reduce_last(0, 0)
    for small in smalls:
        small.wait_recv()
    small_ref[x] = ((smz_ref[0] + smz_ref[1]) + smz_ref[2]) + smz_ref[3]
    small = send(small_ref.at[x], small_ref.at[x], x_peer)
    reduce_last(0, 1)
    for copies in unit.values():
        for copy in copies:
            copy.wait_recv()
    small.wait_recv()
    for copy in started:
        if copy is not ups_copy:
            copy.wait_send()


def fused_local(
    images, upstream, image_count, valid_tokens, qkv_weight, qv_bias, out_weight, out_bias,
    gain_one, shift_one, gain_two, shift_two, up_weight, up_bias, down_weight, down_bias,
):
    rank = lax.axis_index("tensor")
    pad = lambda a: jnp.pad(a, [(0, 0)] * (a.ndim - 1) + [(0, 64)])
    turn = lambda a: jnp.swapaxes(a, 1, 2)
    pack = jnp.stack(
        [
            jnp.concatenate(
                [up_weight, pad(turn(out_weight)), pad(qkv_weight[:, 0])], axis=-1
            ),
            jnp.concatenate(
                [turn(down_weight), pad(qkv_weight[:, 1]), pad(qkv_weight[:, 2])], axis=-1
            ),
        ],
        axis=1,
    )
    pack = jnp.pad(pack, [(0, 0), (0, 0), (0, 8), (0, 0)])
    vecs = jnp.stack(
        [out_bias, gain_one, shift_one, gain_two, shift_two, down_bias, out_bias, out_bias], axis=1
    )
    qvb = pad(take_half(qv_bias, 192, rank))
    upb = take_half(up_bias, 768, rank)[:, None]
    vmem = pl.BlockSpec(memory_space=pltpu.VMEM)
    smem = pl.BlockSpec(memory_space=pltpu.SMEM)
    V = pltpu.VMEM
    output, grad_images, grads, small = pl.pallas_call(
        fused_kernel,
        out_shape=(
            jax.ShapeDtypeStruct((100, 384), F32),
            jax.ShapeDtypeStruct((100, 384), F32),
            jax.ShapeDtypeStruct((2, 2, 24, WIDE), F32),
            jax.ShapeDtypeStruct((2, 16, 768), F32),
        ),
        in_specs=[smem] * 2 + [vmem] * 6,
        out_specs=(vmem,) * 4,
        scratch_shapes=[
            V((2, 2, 4, 2, 48, WIDE), BF),
            V((2, 32, WIDE), BF),
            V((3, ROWS, 384), F32),
            V((2, ROWS, 384), F32),
            V((ROWS, 384), F32),
            V((2, ROWS, 384), BF),
            V((2, ROWS, 384), BF),
            V((2, ROWS, 256), BF),
            V((2, ROWS, 256), BF),
            V((2, ROWS, 256), BF),
            V((2, 3, ROWS, ROWS), F32),
            V((2, ROWS, 256), BF),
            V((2, ROWS, 768), BF),
            V((2, ROWS, 768), F32),
            V((8, ROWS, 384), BF),
            V((8, ROWS, 384), BF),
            V((2, 2, 4, 2, 48, WIDE), BF),
            V((2, 4, 2, 48, WIDE), BF),
            V((2, 4, 2, 48, WIDE), BF),
            V((2, 4, 48, WIDE), BF),
            V((2, 4, 48, WIDE), BF),
            V((2, 3, 48, WIDE), BF),
            V((2, 48, WIDE), F32),
            V((2, 16, 768), F32),
            V((2, 16, 768), F32),
            V((4, 16, 768), F32),
            pltpu.SemaphoreType.DMA((COPIES,)),
            pltpu.SemaphoreType.DMA((COPIES,)),
        ],
        compiler_params=pltpu.CompilerParams(
            collective_id=0, has_side_effects=True, vmem_limit_bytes=48 * 2**20
        ),
        cost_estimate=pl.CostEstimate(
            flops=3 * 10**9, bytes_accessed=2 * 10**7, transcendentals=10**6
        ),
    )(image_count, valid_tokens, images[0], upstream[0], pack, vecs, qvb, upb)
    up_grad = grads[:, 0, :, 0:768]
    out_grad = turn(grads[:, 0, :, 768:960])
    down_grad = turn(grads[:, 1, :, 0:768])
    qkv_grad = jnp.stack(
        [grads[:, 0, :, 1024:1216], grads[:, 1, :, 768:960], grads[:, 1, :, 1024:1216]], axis=1
    )
    small = small.reshape(2, 2, 8, 768)
    up_bias_grad = jnp.concatenate([small[0, :, 0], small[1, :, 0]], axis=-1)
    qv = small[:, :, 1, 0:512].reshape(2, 2, 2, 256)[..., 0:192]
    qv_bias_grad = jnp.concatenate([qv[0], qv[1]], axis=-1)
    row = lambda i, side: small[0, :, i, 384 * side : 384 * side + 384]
    return (
        output[None], grad_images[None], qkv_grad, qv_bias_grad, out_grad, row(2, 0),
        row(2, 1), row(3, 0), row(3, 1), row(4, 0), up_grad, up_bias_grad, down_grad, row(4, 1),
    )

def solution(mesh):
    in_specs = (
        P("fsdp", "tensor", None),
        P("fsdp", "tensor", None),
        P("fsdp"),
        P("fsdp"),
        P(None, None, "fsdp", "tensor"),
        P(),
        P(None, "tensor", "fsdp"),
        P(),
        P(),
        P(),
        P(),
        P(),
        P(None, "fsdp", "tensor"),
        P(),
        P(None, "tensor", "fsdp"),
        P(),
    )
    out_specs = (
        P("fsdp", "tensor", None),
        P("fsdp", "tensor", None),
        P(None, None, "fsdp", "tensor"),
        P(),
        P(None, "tensor", "fsdp"),
        P(),
        P(),
        P(),
        P(),
        P(),
        P(None, "fsdp", "tensor"),
        P(),
        P(None, "tensor", "fsdp"),
        P(),
    )
    body = fused_local if mesh.shape["fsdp"] == 16 else local
    return jax.shard_map(body, mesh=mesh, in_specs=in_specs, out_specs=out_specs, check_vma=False)
```

```python
from functools import partial

import jax
import jax.numpy as jnp
from jax import lax
from jax.experimental import pallas as pl
from jax.experimental.pallas import tpu as pltpu
from jax.sharding import PartitionSpec as P

D = 384
HD = 64
FF = 1536


epsilon = 1e-06


def norm_rows(hidden, gain, shift):
    centre = hidden - jnp.mean(hidden, axis=-1, keepdims=True)
    spread = jnp.mean(centre * centre, axis=-1, keepdims=True)
    return centre * lax.rsqrt(spread + epsilon) * gain + shift


def take_half(vector, width_here, index):
    return lax.dynamic_slice_in_dim(vector, index * width_here, width_here, vector.ndim - 1)


def widen_half(vector, index, total):
    empty = jnp.zeros(vector.shape[:-1] + (total,), jnp.float32)
    return lax.dynamic_update_slice_in_dim(empty, vector, index * vector.shape[-1], vector.ndim - 1)


def head_split(array):
    slot_count, length, head_width = array.shape
    return array.reshape(slot_count, length, head_width // HD, HD)


def masked_scores(queries, key_rows, key_ok):
    scores = jnp.einsum(
        "sqhd,skhd->shqk",
        head_split(queries),
        head_split(key_rows),
        preferred_element_type=jnp.float32,
    ) * HD ** (-0.5)
    return jnp.where(key_ok[:, None, None, :], scores, -1e30)


def attend(queries, key_rows, values, key_ok):
    scores = masked_scores(queries, key_rows, key_ok)
    highest_score = jnp.max(scores, axis=-1, keepdims=True)
    log_total = highest_score + jnp.log(
        jnp.sum(jnp.exp(scores - highest_score), axis=-1, keepdims=True)
    )
    portions = jnp.exp(scores - log_total).astype(jnp.bfloat16)
    mixed = jnp.einsum(
        "shqk,skhd->sqhd", portions, head_split(values), preferred_element_type=jnp.float32
    )
    return (log_total, mixed.reshape(queries.shape).astype(jnp.bfloat16))


def attend_back(queries, key_rows, values, log_total, grad_mixed, key_ok):
    portions = jnp.exp(masked_scores(queries, key_rows, key_ok) - log_total)
    grad_heads = head_split(grad_mixed)
    grad_portions = jnp.einsum(
        "sqhd,skhd->shqk", grad_heads, head_split(values), preferred_element_type=jnp.float32
    )
    grad_values = jnp.einsum(
        "shqk,sqhd->skhd",
        portions.astype(jnp.bfloat16),
        grad_heads,
        preferred_element_type=jnp.float32,
    )
    inner_sum = jnp.sum(portions * grad_portions, axis=-1, keepdims=True)
    grad_scores = (portions * (grad_portions - inner_sum)).astype(jnp.bfloat16)
    grad_queries = jnp.einsum(
        "shqk,skhd->sqhd", grad_scores, head_split(key_rows), preferred_element_type=jnp.float32
    ) * HD ** (-0.5)
    grad_keys = jnp.einsum(
        "shqk,sqhd->skhd", grad_scores, head_split(queries), preferred_element_type=jnp.float32
    ) * HD ** (-0.5)
    full_shape = queries.shape
    return (
        grad_queries.reshape(full_shape).astype(jnp.bfloat16),
        grad_keys.reshape(full_shape).astype(jnp.bfloat16),
        grad_values.reshape(full_shape).astype(jnp.bfloat16),
    )


def fetch_weights(qkv_part, out_part, up_part, down_part):
    return (
        lax.all_gather(qkv_part, "fsdp", axis=1, tiled=True),
        lax.all_gather(out_part, "fsdp", axis=1, tiled=True),
        lax.all_gather(up_part, "fsdp", axis=0, tiled=True),
        lax.all_gather(down_part, "fsdp", axis=1, tiled=True),
    )


def share_tokens(value):
    return lax.all_gather(value, "tensor", axis=1, tiled=True)


def sum_branch(value):
    return lax.psum_scatter(
        value.astype(jnp.bfloat16), "tensor", scatter_dimension=1, tiled=True
    ).astype(jnp.float32)


def gather_grads(value):
    return lax.all_gather(value, "tensor", axis=1, tiled=True)


def sum_inputs(value):
    return lax.psum_scatter(
        value.astype(jnp.bfloat16), "tensor", scatter_dimension=1, tiled=True
    ).astype(jnp.float32)


def local(
    images,
    upstream,
    image_count,
    valid_tokens,
    qkv_weight,
    qv_bias,
    out_weight,
    out_bias,
    gain_one,
    shift_one,
    gain_two,
    shift_two,
    up_weight,
    up_bias,
    down_weight,
    down_bias,
):
    slot_count, half_length, model_width = images.shape
    tensor_size = lax.axis_size("tensor")
    tensor_rank = lax.axis_index("tensor")
    length = half_length * tensor_size
    head_width = qkv_weight.shape[3]
    hidden_width = up_weight.shape[2]
    layer_count = qkv_weight.shape[0]
    key_ok = jnp.arange(length, dtype=jnp.int32)[None, :] < valid_tokens[:, None]
    slot_live = jnp.arange(slot_count, dtype=jnp.int32) < image_count[0]
    own_rows = tensor_rank * half_length + jnp.arange(half_length, dtype=jnp.int32)
    row_ok = jnp.where(
        (own_rows[None, :] < valid_tokens[:, None]) & slot_live[:, None], 1.0, 0.0
    ).astype(jnp.float32)
    stored = []
    hidden = images
    for layer_index in range(layer_count):
        fetched = fetch_weights(
            qkv_weight[layer_index],
            out_weight[layer_index],
            up_weight[layer_index],
            down_weight[layer_index],
        )
        qkv_full, out_full, up_full, down_full = fetched
        bias_pair = take_half(qv_bias[layer_index], head_width, tensor_rank)
        normed = norm_rows(hidden, gain_one[layer_index], shift_one[layer_index]).astype(
            jnp.bfloat16
        )
        shared = share_tokens(normed)
        project = jnp.einsum("std,cde->cste", shared, qkv_full, preferred_element_type=jnp.float32)
        queries = (project[0] + bias_pair[0]).astype(jnp.bfloat16)
        key_rows = project[1].astype(jnp.bfloat16)
        values = (project[2] + bias_pair[1]).astype(jnp.bfloat16)
        log_total, mixed = attend(queries, key_rows, values, key_ok)
        branch = sum_branch(
            jnp.einsum("ste,ed->std", mixed, out_full, preferred_element_type=jnp.float32)
        )
        middle = hidden + (branch + out_bias[layer_index])
        normed_two = norm_rows(middle, gain_two[layer_index], shift_two[layer_index]).astype(
            jnp.bfloat16
        )
        shared_two = share_tokens(normed_two)
        up_value = jnp.einsum(
            "std,df->stf", shared_two, up_full, preferred_element_type=jnp.float32
        ) + take_half(up_bias[layer_index], hidden_width, tensor_rank)
        activated = jax.nn.gelu(up_value, approximate=False).astype(jnp.bfloat16)
        branch_two = sum_branch(
            jnp.einsum("stf,fd->std", activated, down_full, preferred_element_type=jnp.float32)
        )
        stored.append(
            (
                hidden,
                shared,
                queries,
                key_rows,
                values,
                log_total,
                mixed,
                middle,
                shared_two,
                up_value,
                activated,
                fetched,
            )
        )
        hidden = middle + (branch_two + down_bias[layer_index])
    output = hidden * row_ok[:, :, None]
    grad_hidden = upstream * row_ok[:, :, None]
    large_grads = [None] * layer_count
    small_grads = [None] * layer_count
    for layer_index in reversed(range(layer_count)):
        (
            hidden_in,
            shared,
            queries,
            key_rows,
            values,
            log_total,
            mixed,
            middle,
            shared_two,
            up_value,
            activated,
            fetched,
        ) = stored[layer_index]
        qkv_full, out_full, up_full, down_full = (
            lax.all_gather(qkv_weight[layer_index], "fsdp", axis=1, tiled=True),
            lax.all_gather(out_weight[layer_index], "fsdp", axis=1, tiled=True),
            lax.all_gather(up_weight[layer_index], "fsdp", axis=0, tiled=True),
            lax.all_gather(down_weight[layer_index], "fsdp", axis=1, tiled=True),
        )
        grad_branch = grad_hidden.astype(jnp.bfloat16)
        down_bias_grad = jnp.sum(grad_branch.astype(jnp.float32), axis=(0, 1))
        grad_rows = gather_grads(grad_branch)
        down_grad = jnp.einsum(
            "stf,std->fd", activated, grad_rows, preferred_element_type=jnp.float32
        )
        grad_activated = jnp.einsum(
            "std,fd->stf", grad_rows, down_full, preferred_element_type=jnp.float32
        )
        gelu_back = jax.vjp(partial(jax.nn.gelu, approximate=False), up_value)[1]
        grad_up = gelu_back(grad_activated)[0].astype(jnp.bfloat16)
        up_bias_grad = widen_half(
            jnp.sum(grad_up.astype(jnp.float32), axis=(0, 1)), tensor_rank, FF
        )
        up_grad = jnp.einsum("std,stf->df", shared_two, grad_up, preferred_element_type=jnp.float32)
        grad_normed_two = sum_inputs(
            jnp.einsum("stf,df->std", grad_up, up_full, preferred_element_type=jnp.float32)
        )
        norm_back = jax.vjp(norm_rows, middle, gain_two[layer_index], shift_two[layer_index])[1]
        grad_from_norm, gain_two_grad, shift_two_grad = norm_back(grad_normed_two)
        grad_middle = grad_hidden + grad_from_norm
        grad_branch = grad_middle.astype(jnp.bfloat16)
        out_bias_grad = jnp.sum(grad_branch.astype(jnp.float32), axis=(0, 1))
        grad_rows = gather_grads(grad_branch)
        out_grad = jnp.einsum("ste,std->ed", mixed, grad_rows, preferred_element_type=jnp.float32)
        grad_mixed = jnp.einsum(
            "std,ed->ste", grad_rows, out_full, preferred_element_type=jnp.float32
        ).astype(jnp.bfloat16)
        grad_queries, grad_keys, grad_values = attend_back(
            queries, key_rows, values, log_total, grad_mixed, key_ok
        )
        grad_project = jnp.stack([grad_queries, grad_keys, grad_values])
        qkv_grad = jnp.einsum(
            "std,cste->cde", shared, grad_project, preferred_element_type=jnp.float32
        )
        qv_sums = jnp.stack(
            [
                jnp.sum(grad_queries.astype(jnp.float32), axis=(0, 1)),
                jnp.sum(grad_values.astype(jnp.float32), axis=(0, 1)),
            ]
        )
        qv_bias_grad = widen_half(qv_sums, tensor_rank, D)
        grad_normed = sum_inputs(
            jnp.einsum("cste,cde->std", grad_project, qkv_full, preferred_element_type=jnp.float32)
        )
        norm_back = jax.vjp(norm_rows, hidden_in, gain_one[layer_index], shift_one[layer_index])[1]
        grad_input, gain_one_grad, shift_one_grad = norm_back(grad_normed)
        grad_hidden = grad_middle + grad_input
        large_grads[layer_index] = (
            lax.psum_scatter(qkv_grad, "fsdp", scatter_dimension=1, tiled=True),
            lax.psum_scatter(out_grad, "fsdp", scatter_dimension=1, tiled=True),
            lax.psum_scatter(up_grad, "fsdp", scatter_dimension=0, tiled=True),
            lax.psum_scatter(down_grad, "fsdp", scatter_dimension=1, tiled=True),
        )
        small_grads[layer_index] = (
            qv_bias_grad,
            out_bias_grad,
            gain_one_grad,
            shift_one_grad,
            gain_two_grad,
            shift_two_grad,
            up_bias_grad,
            down_bias_grad,
        )
    stacked = tuple(
        (
            jnp.stack([large_grads[layer_index][member] for layer_index in range(layer_count)])
            for member in range(4)
        )
    )
    small_stacked = tuple(
        (
            jnp.stack([small_grads[layer_index][member] for layer_index in range(layer_count)])
            for member in range(8)
        )
    )
    summed = lax.psum(
        (
            small_stacked[0],
            small_stacked[1],
            small_stacked[2],
            small_stacked[3],
            small_stacked[4],
            small_stacked[5],
            small_stacked[6],
            small_stacked[7],
        ),
        ("fsdp", "tensor"),
    )
    return (
        output,
        grad_hidden,
        stacked[0],
        summed[0],
        stacked[1],
        summed[1],
        summed[2],
        summed[3],
        summed[4],
        summed[5],
        stacked[2],
        summed[6],
        stacked[3],
        summed[7],
    )


BF = jnp.bfloat16
F32 = jnp.float32
HALF = 112
ROWS = 2 * HALF
WIDE = 1280
FFN = pl.ds(0, 768)
ATT = pl.ds(768, 512)
PARTS = (FFN, ATT)
COPIES = 90


def dot(a, b, ca, cb):
    return lax.dot_general(a, b, (((ca,), (cb,)), ((), ())), preferred_element_type=F32)


def row_stats(x):
    centre = x - jnp.mean(x, axis=-1, keepdims=True)
    r = lax.rsqrt(jnp.mean(centre * centre, axis=-1, keepdims=True) + epsilon)
    return centre * r, r


def norm_grad(e, xhat, r, gain):
    gy = e * gain
    return r * (
        gy
        - jnp.mean(gy, axis=-1, keepdims=True)
        - xhat * jnp.mean(gy * xhat, axis=-1, keepdims=True)
    )


def col_sum(x):
    return jnp.sum(x, axis=0, keepdims=True)


def fused_kernel(
    count_ref, valid_ref, img_ref, ups_ref, pack_ref, vec_ref, qvb_ref, upb_ref,
    out_ref, gimg_ref, gw_ref, small_ref, late_sum_ref,
    late_ref, late_out_ref,
    own_ref, tok_ref, w_ref, pr_ref, hid_ref, mid_ref, g_ref, n1_ref, n2_ref, q_ref, k_ref, v_ref, p_ref,
    mix_ref, act_ref, dg_ref, xs_ref, xr_ref, gs_ref, r1_ref, s1_ref, r2_ref, s2_ref,
    r3_ref, s3_ref, sm_ref, smr_ref, smz_ref, send_sem, recv_sem,
):
    f = lax.axis_index("fsdp")
    x = lax.axis_index("tensor")
    c = lax.rem(f, 2)
    y = lax.rem(f // 2, 2)
    z = f // 4

    def at(zz, yy, cc):
        return {"fsdp": zz * 4 + yy * 2 + cc}

    core_peer = at(z, y, 1 - c)
    y_peer = at(z, 1 - y, c)
    x_peer = {"tensor": 1 - x}
    z_next = [lax.rem(z + d, 4) for d in range(4)]
    z_from = [lax.rem(z + 4 - d, 4) for d in range(4)]

    barrier = pltpu.get_barrier_semaphore()
    greeted = [core_peer, y_peer, x_peer] + [at(z_next[d], y, c) for d in (1, 2, 3)]
    over_zx = [x_peer] + [{**at(z_next[d], y, c), "tensor": t} for d in (1, 2, 3) for t in (x, 1 - x)]
    over_yc = [core_peer, y_peer, at(z, 1 - y, 1 - c)]
    greeted += over_zx[2::2] + over_yc[2:]
    for peer in greeted:
        pl.semaphore_signal(barrier, inc=1, device_id=peer, device_id_type=pl.DeviceIdType.MESH)
    pl.semaphore_wait(barrier, len(greeted))

    started = []

    def send(src, dst, peer):
        i = len(started)
        copy = pltpu.make_async_remote_copy(
            src_ref=src, dst_ref=dst, send_sem=send_sem.at[i], recv_sem=recv_sem.at[i],
            device_id=peer, device_id_type=pl.DeviceIdType.MESH,
        )
        copy.start()
        started.append(copy)
        return copy

    pack_copies = [send(pack_ref.at[l, 1 - c], pr_ref.at[l], core_peer) for l in range(2)]

    own_row = lax.broadcasted_iota(jnp.int32, (HALF, 1), 0)
    valid = valid_ref[0]
    own_ok = (own_row < 100) & (x * 100 + own_row < valid) & (count_ref[0] > 0)
    row_ok = jnp.where(own_ok, 1.0, 0.0).astype(F32)
    own_ref[...] = jnp.zeros((2, HALF, 384), F32)
    own_ref[0, 0:100] = img_ref[...]
    own_ref[1, 0:100] = ups_ref[...]
    hid_ref[0, 0:HALF] = own_ref[0]
    tok_ref[0, 0] = own_ref[0].astype(BF)
    img_copy = send(tok_ref.at[0, 0], tok_ref.at[0, 1], x_peer)

    z_copies, y_copies, c_copies = {}, {}, {}
    for l in range(2):
        pack_copies[l].wait_recv()
        mine = pack_ref[l, c].astype(F32)[:24]
        theirs = pr_ref[l].astype(F32)[:24]
        first = jnp.broadcast_to(c, mine.shape) == 0
        chunk = jnp.concatenate(
            [jnp.where(first, mine, theirs), jnp.where(first, theirs, mine)], axis=0
        )
        w_ref[l, c, z, y] = chunk.astype(BF)

    def gather_z(l, a):
        block = w_ref.at[l, c, z, y, :, PARTS[a]]
        z_copies[l, a] = [send(block, block, at(z_next[d], y, c)) for d in (1, 2, 3)]
        y_copies[l, a] = [send(block, block, y_peer)]

    gather_z(0, 1)
    gather_z(0, 0)

    def ups_start():
        own = own_ref[1] * row_ok
        g_ref[0:HALF] = own
        tok_ref[1, 0] = own.astype(BF)
        return send(tok_ref.at[1, 0], tok_ref.at[1, 1], x_peer)

    def gather_y(l, a):
        for d in (1, 2, 3):
            z_copies[l, a][d - 1].wait_recv()
            block = w_ref.at[l, c, z_from[d], y, :, PARTS[a]]
            y_copies[l, a].append(send(block, block, y_peer))

    def gather_core(l, a):
        for copy in y_copies[l, a]:
            copy.wait_recv()
        block = w_ref.at[l, c, :, :, :, PARTS[a]]
        c_copies[l, a] = send(block, block, core_peer)

    def gather_end(l, a):
        c_copies[l, a].wait_recv()

    def kept_rows(i):
        return HALF if i in (3, 7) else ROWS

    def x_start(i, value):
        xs_ref[i] = value.astype(BF)
        copies = [send(xs_ref.at[i, HALF:ROWS], xr_ref.at[i, 0:HALF], x_peer)]
        if kept_rows(i) == ROWS:
            copies.append(send(xs_ref.at[i, 0:HALF], xr_ref.at[i, HALF:ROWS], x_peer))
        return copies

    def x_end(i, copies):
        for copy in copies:
            copy.wait_recv()
        kept = kept_rows(i)
        return xs_ref[i, 0:kept].astype(F32) + xr_ref[i, 0:kept].astype(F32)

    def weight(l, half, start, size):
        return w_ref[l, half, :, :, :, pl.ds(start, size)].reshape(384, size)

    def vec(l, i):
        return vec_ref[l, i : i + 1]

    lane = lax.broadcasted_iota(jnp.int32, (ROWS, 256), 1)
    head_mask = [
        jnp.where((lane >= HD * h) & (lane < HD * h + HD), 1.0, 0.0).astype(F32).astype(BF)
        for h in range(3)
    ]
    key = lax.broadcasted_iota(jnp.int32, (ROWS, ROWS), 1)
    in_half = jnp.where(key < HALF, key, key - HALF)
    token = in_half + 100 * jnp.where(key < HALF, x, 1 - x)
    key_ok = (in_half < 100) & (token < valid)

    def attention(l):
        xhat, r = row_stats(hid_ref[l])
        n1 = (xhat * vec(l, 1) + vec(l, 2)).astype(BF)
        n1_ref[l] = n1
        yield
        q = (dot(n1, weight(l, 0, 1024, 256), 1, 0) + qvb_ref[l, 0:1]).astype(BF)
        k = dot(n1, weight(l, 1, 768, 256), 1, 0).astype(BF)
        v = (dot(n1, weight(l, 1, 1024, 256), 1, 0) + qvb_ref[l, 1:2]).astype(BF)
        q_ref[l], k_ref[l], v_ref[l] = q, k, v
        mixed = jnp.zeros((ROWS, 256), F32)
        for h in range(3):
            scores = jnp.where(key_ok, dot(q * head_mask[h], k, 1, 1) * HD ** (-0.5), -1e30)
            e = jnp.exp(scores - jnp.max(scores, axis=-1, keepdims=True))
            p = e / jnp.sum(e, axis=-1, keepdims=True)
            p_ref[l, h] = p
            mixed = mixed + dot(p.astype(BF), v * head_mask[h], 1, 0)
        mix_ref[l] = mixed.astype(BF)
        copies = x_start(2 * l, dot(mix_ref[l], weight(l, 0, 768, 256), 1, 1))
        yield
        branch = x_end(2 * l, copies)
        mid_ref[l] = hid_ref[l] + (branch + vec(l, 0))

    def feed(l):
        xhat, r = row_stats(mid_ref[l])
        n2 = (xhat * vec(l, 3) + vec(l, 4)).astype(BF)
        n2_ref[l] = n2
        yield
        up = dot(n2, weight(l, 0, 0, 768), 1, 0) + upb_ref[l]
        phi = 0.5 * (1.0 + lax.erf(up * (0.5**0.5)))
        act_ref[l] = (up * phi).astype(BF)
        dg_ref[l] = phi + up * (jnp.exp(-0.5 * up * up) * 0.3989422804014327)
        copies = x_start(2 * l + 1, dot(act_ref[l], weight(l, 1, 0, 768), 1, 1))
        yield
        branch = x_end(2 * l + 1, copies)
        kept = kept_rows(2 * l + 1)
        hid_ref[l + 1, 0:kept] = mid_ref[l, 0:kept] + (branch + vec(l, 5))

    gather_y(0, 1)
    gather_z(1, 1)
    img_copy.wait_recv()
    hid_ref[0, HALF:ROWS] = tok_ref[0, 1].astype(F32)
    ups_copy = ups_start()
    step = attention(0)
    next(step)
    gather_y(0, 0)
    gather_core(0, 1)
    gather_z(1, 0)
    gather_end(0, 1)
    next(step)
    gather_y(1, 1)
    gather_core(0, 0)
    next(step, None)
    step = feed(0)
    next(step)
    gather_end(0, 0)
    next(step)
    gather_y(1, 0)
    gather_core(1, 1)
    next(step, None)
    step = attention(1)
    next(step)
    gather_end(1, 1)
    next(step)
    gather_core(1, 0)
    next(step, None)
    step = feed(1)
    next(step)
    gather_end(1, 0)
    next(step)
    next(step, None)
    out_ref[...] = (hid_ref[2, 0:HALF] * row_ok)[0:100]
    ups_copy.wait_recv()
    g_ref[HALF:ROWS] = tok_ref[1, 1].astype(F32)

    unit = {}

    def reduce_core(l, a):
        part = PARTS[a]
        unit[l, a] = [
            send(gs_ref.at[l, 1 - c, :, :, :, part], r1_ref.at[l, :, :, :, part], core_peer)
        ]

    def reduce_y(l, a):
        part = PARTS[a]
        unit[l, a][0].wait_recv()
        total = gs_ref[l, c, :, :, :, part].astype(F32) + r1_ref[l, :, :, :, part].astype(F32)
        s1_ref[l, :, :, :, part] = total.astype(BF)
        unit[l, a] = [send(s1_ref.at[l, :, 1 - y, :, part], r2_ref.at[l, :, :, part], y_peer)]

    def reduce_z(l, a):
        part = PARTS[a]
        unit[l, a][0].wait_recv()
        total = s1_ref[l, :, y, :, part].astype(F32) + r2_ref[l, :, :, part].astype(F32)
        s2_ref[l, :, :, part] = total.astype(BF)
        unit[l, a] = [
            send(
                s2_ref.at[l, z_next[d], :, part], r3_ref.at[l, d - 1, :, part],
                at(z_next[d], y, c),
            )
            for d in (1, 2, 3)
        ]

    def reduce_last(l, a):
        part = PARTS[a]
        for copy in unit[l, a]:
            copy.wait_recv()
        total = s2_ref[l, z, :, part].astype(F32)
        for d in range(3):
            total = total + r3_ref[l, d, :, part].astype(F32)
        s3_ref[l, :, part] = total
        other = pl.ds(pl.multiple_of(24 * (1 - c), 8), 24)
        own = pl.ds(pl.multiple_of(24 * c, 8), 24)
        unit[l, a] = [send(s3_ref.at[l, other, part], gw_ref.at[l, c, :, part], core_peer)]
        gw_ref[l, c, :, part] = s3_ref[l, own, part]

    def keep(l, half, start, value):
        size = value.shape[1]
        gs_ref[l, half, :, :, :, pl.ds(start, size)] = value.astype(BF).reshape(4, 2, 48, size)

    def feed_back(l):
        g = g_ref[...]
        gb = g.astype(BF)
        ga = dot(gb, weight(l, 1, 0, 768), 1, 0)
        gu = (ga * dg_ref[l]).astype(BF)
        copies = x_start(6 - 2 * l, dot(gu, weight(l, 0, 0, 768), 1, 1))
        keep(l, 1, 0, dot(gb, act_ref[l], 0, 0))
        keep(l, 0, 0, dot(n2_ref[l], gu, 0, 0))
        reduce_core(l, 0)
        yield
        sm_ref[0, 8 * l : 8 * l + 1, :] = col_sum(gu.astype(F32))
        sm_ref[0, 8 * l + 4 : 8 * l + 5, 384:768] = col_sum(gb.astype(F32))
        xhat, r = row_stats(mid_ref[l])
        e = x_end(6 - 2 * l, copies)
        sm_ref[0, 8 * l + 3 : 8 * l + 4, 384:768] = col_sum(e * xhat)
        sm_ref[0, 8 * l + 4 : 8 * l + 5, 0:384] = col_sum(e)
        g_ref[...] = g + norm_grad(e, xhat, r, vec(l, 3))

    def attention_back(l):
        g = g_ref[...]
        gm = g.astype(BF)
        q, k, v = q_ref[l], k_ref[l], v_ref[l]
        gmix = dot(gm, weight(l, 0, 768, 256), 1, 0).astype(BF)
        gq = jnp.zeros((ROWS, 256), F32)
        gk, gv = gq, gq
        for h in range(3):
            p = p_ref[l, h]
            gmh = gmix * head_mask[h]
            dp = dot(gmh, v, 1, 1)
            gv = gv + dot(p.astype(BF), gmh, 0, 0)
            ds = (p * (dp - jnp.sum(p * dp, axis=-1, keepdims=True))).astype(BF)
            gq = gq + dot(ds, k * head_mask[h], 1, 0)
            gk = gk + dot(ds, q * head_mask[h], 0, 0)
        gq = (gq * HD ** (-0.5)).astype(BF)
        gk = (gk * HD ** (-0.5)).astype(BF)
        gv = gv.astype(BF)
        copies = x_start(
            7 - 2 * l,
            dot(gq, weight(l, 0, 1024, 256), 1, 1)
            + dot(gk, weight(l, 1, 768, 256), 1, 1)
            + dot(gv, weight(l, 1, 1024, 256), 1, 1),
        )
        n1 = n1_ref[l]
        keep(l, 0, 768, dot(gm, mix_ref[l], 0, 0))
        keep(l, 0, 1024, dot(n1, gq, 0, 0))
        keep(l, 1, 768, dot(n1, gk, 0, 0))
        keep(l, 1, 1024, dot(n1, gv, 0, 0))
        reduce_core(l, 1)
        yield
        first_sums = [col_sum(v.astype(F32)) for v in (gq, gv, gm)]
        kept = kept_rows(7 - 2 * l)
        xhat, r = row_stats(hid_ref[l, 0:kept])
        e = x_end(7 - 2 * l, copies)
        sums = first_sums + [col_sum(e * xhat), col_sum(e)]
        if l == 0:
            at_row = 0
            for total in sums:
                for i in range(total.shape[1] // 128):
                    late_ref[f_zx, at_row : at_row + 1] = total[:, 128 * i : 128 * i + 128]
                    at_row += 1
        else:
            sm_ref[0, 9:10, 0:256] = sums[0]
            sm_ref[0, 9:10, 256:512] = sums[1]
            sm_ref[0, 10:11, 0:384] = sums[2]
            sm_ref[0, 10:11, 384:768] = sums[3]
            sm_ref[0, 11:12, 0:384] = sums[4]
        g_ref[0:kept] = g[0:kept] + norm_grad(e, xhat, r, vec(l, 1))

    sm_ref[0] = jnp.zeros((16, 768), F32)
    f_zx = z * 2 + x
    f_yc = y * 2 + c
    late_ref[f_zx] = jnp.zeros((24, 128), F32)
    step = feed_back(1)
    next(step)
    next(step, None)
    reduce_y(1, 0)
    step = attention_back(1)
    next(step)
    next(step, None)
    reduce_y(1, 1)
    reduce_z(1, 0)
    step = feed_back(0)
    next(step)
    next(step, None)
    reduce_y(0, 0)
    reduce_z(1, 1)
    small = send(sm_ref.at[0], smr_ref.at[0], core_peer)
    step = attention_back(0)
    next(step)
    small.wait_recv()
    sm_ref[1] = sm_ref[0] + smr_ref[0]
    small = send(sm_ref.at[1], smr_ref.at[1], y_peer)
    reduce_z(0, 0)
    reduce_y(0, 1)
    small.wait_recv()
    smz_ref[z] = sm_ref[1] + smr_ref[1]
    smalls = [send(smz_ref.at[z], smz_ref.at[z], at(z_next[d], y, c)) for d in (1, 2, 3)]
    next(step, None)
    lates = [send(late_ref.at[f_zx], late_ref.at[f_zx], peer) for peer in over_zx]
    reduce_last(1, 0)
    reduce_last(1, 1)
    reduce_z(0, 1)
    for small in smalls:
        small.wait_recv()
    small_ref[x] = ((smz_ref[0] + smz_ref[1]) + smz_ref[2]) + smz_ref[3]
    small = send(small_ref.at[x], small_ref.at[x], x_peer)
    for late in lates:
        late.wait_recv()
    for t in range(2):
        total = late_ref[t]
        for zz in range(1, 4):
            total = total + late_ref[2 * zz + t]
        late_out_ref[f_yc, t] = total
    lates = [send(late_out_ref.at[f_yc], late_out_ref.at[f_yc], peer) for peer in over_yc]
    gimg_ref[...] = g_ref[0:HALF][0:100]
    reduce_last(0, 0)
    reduce_last(0, 1)
    for late in lates:
        late.wait_recv()
    late_sum_ref[...] = (late_out_ref[0] + late_out_ref[1]) + (late_out_ref[2] + late_out_ref[3])
    for copies in unit.values():
        for copy in copies:
            copy.wait_recv()
    small.wait_recv()
    for copy in started:
        copy.wait_send()


def unpack_kernel(
    output_in, gimg_in, gw_in, small_in, late_in,
    output, gimg, qkv, qv, out_grad, out_bias, gain_one, shift_one, gain_two, shift_two,
    up_grad, up_bias, down_grad, down_bias,
):
    output[...] = output_in[...]
    gimg[...] = gimg_in[...]
    for l in range(2):
        up_grad[l] = gw_in[l, 0, :, 0:768]
        down_grad[l] = gw_in[l, 1, :, 0:768].T
        out_grad[l] = gw_in[l, 0, :, 768:1024].T[0:192]
        qkv[l, 0] = gw_in[l, 0, :, 1024:1216]
        qkv[l, 1] = gw_in[l, 1, :, 768:960]
        qkv[l, 2] = gw_in[l, 1, :, 1024:1216]
        row = 8 * l
        for t in range(2):
            up_bias[l : l + 1, 768 * t : 768 * t + 768] = small_in[t, row : row + 1, :]
        gain_two[l : l + 1] = small_in[0, row + 3 : row + 4, 384:768]
        shift_two[l : l + 1] = small_in[0, row + 4 : row + 5, 0:384]
        down_bias[l : l + 1] = small_in[0, row + 4 : row + 5, 384:768]
    for t in range(2):
        for i in range(2):
            qv[0, i : i + 1, 192 * t : 192 * t + 128] = late_in[t, 2 * i : 2 * i + 1, :]
            qv[0, i : i + 1, 192 * t + 128 : 192 * t + 192] = late_in[t, 2 * i + 1 : 2 * i + 2, 0:64]
            qv[1, i : i + 1, 192 * t : 192 * t + 192] = small_in[t, 9:10, 256 * i : 256 * i + 192]
    for i in range(3):
        lanes = slice(128 * i, 128 * i + 128)
        out_bias[0:1, lanes] = late_in[0, 4 + i : 5 + i, :]
        gain_one[0:1, lanes] = late_in[0, 7 + i : 8 + i, :] + late_in[1, 7 + i : 8 + i, :]
        shift_one[0:1, lanes] = late_in[0, 10 + i : 11 + i, :] + late_in[1, 10 + i : 11 + i, :]
    out_bias[1:2] = small_in[0, 10:11, 0:384]
    gain_one[1:2] = small_in[0, 10:11, 384:768]
    shift_one[1:2] = small_in[0, 11:12, 0:384]


def fused_local(
    images, upstream, image_count, valid_tokens, qkv_weight, qv_bias, out_weight, out_bias,
    gain_one, shift_one, gain_two, shift_two, up_weight, up_bias, down_weight, down_bias,
):
    rank = lax.axis_index("tensor")
    pad = lambda a: jnp.pad(a, [(0, 0)] * (a.ndim - 1) + [(0, 64)])
    turn = lambda a: jnp.swapaxes(a, 1, 2)
    pack = jnp.stack(
        [
            jnp.concatenate(
                [up_weight, pad(turn(out_weight)), pad(qkv_weight[:, 0])], axis=-1
            ),
            jnp.concatenate(
                [turn(down_weight), pad(qkv_weight[:, 1]), pad(qkv_weight[:, 2])], axis=-1
            ),
        ],
        axis=1,
    )
    pack = jnp.pad(pack, [(0, 0), (0, 0), (0, 8), (0, 0)])
    vecs = jnp.stack(
        [out_bias, gain_one, shift_one, gain_two, shift_two, down_bias, out_bias, out_bias], axis=1
    )
    qvb = pad(take_half(qv_bias, 192, rank))
    upb = take_half(up_bias, 768, rank)[:, None]
    vmem = pl.BlockSpec(memory_space=pltpu.VMEM)
    smem = pl.BlockSpec(memory_space=pltpu.SMEM)
    V = pltpu.VMEM
    output, grad_images, grads, small, late = pl.pallas_call(
        fused_kernel,
        out_shape=(
            jax.ShapeDtypeStruct((100, 384), F32),
            jax.ShapeDtypeStruct((100, 384), F32),
            jax.ShapeDtypeStruct((2, 2, 24, WIDE), F32),
            jax.ShapeDtypeStruct((2, 16, 768), F32),
            jax.ShapeDtypeStruct((2, 24, 128), F32),
        ),
        in_specs=[smem] * 2 + [vmem] * 6,
        out_specs=(vmem,) * 5,
        scratch_shapes=[
            V((8, 24, 128), F32),
            V((4, 2, 24, 128), F32),
            V((2, HALF, 384), F32),
            V((2, 2, HALF, 384), BF),
            V((2, 2, 4, 2, 48, WIDE), BF),
            V((2, 32, WIDE), BF),
            V((3, ROWS, 384), F32),
            V((2, ROWS, 384), F32),
            V((ROWS, 384), F32),
            V((2, ROWS, 384), BF),
            V((2, ROWS, 384), BF),
            V((2, ROWS, 256), BF),
            V((2, ROWS, 256), BF),
            V((2, ROWS, 256), BF),
            V((2, 3, ROWS, ROWS), F32),
            V((2, ROWS, 256), BF),
            V((2, ROWS, 768), BF),
            V((2, ROWS, 768), F32),
            V((8, ROWS, 384), BF),
            V((8, ROWS, 384), BF),
            V((2, 2, 4, 2, 48, WIDE), BF),
            V((2, 4, 2, 48, WIDE), BF),
            V((2, 4, 2, 48, WIDE), BF),
            V((2, 4, 48, WIDE), BF),
            V((2, 4, 48, WIDE), BF),
            V((2, 3, 48, WIDE), BF),
            V((2, 48, WIDE), F32),
            V((2, 16, 768), F32),
            V((2, 16, 768), F32),
            V((4, 16, 768), F32),
            pltpu.SemaphoreType.DMA((COPIES,)),
            pltpu.SemaphoreType.DMA((COPIES,)),
        ],
        compiler_params=pltpu.CompilerParams(
            collective_id=0, has_side_effects=True, vmem_limit_bytes=48 * 2**20
        ),
        cost_estimate=pl.CostEstimate(
            flops=3 * 10**9, bytes_accessed=2 * 10**7, transcendentals=10**6
        ),
    )(image_count, valid_tokens, images[0], upstream[0], pack, vecs, qvb, upb)
    shapes = [
        (100, 384), (100, 384), (2, 3, 24, 192), (2, 2, 384), (2, 192, 24), (2, 384), (2, 384),
        (2, 384), (2, 384), (2, 384), (2, 24, 768), (2, 1536), (2, 768, 24), (2, 384),
    ]
    results = pl.pallas_call(
        unpack_kernel,
        out_shape=[jax.ShapeDtypeStruct(shape, F32) for shape in shapes],
        in_specs=[vmem] * 5,
        out_specs=[vmem] * 14,
        compiler_params=pltpu.CompilerParams(vmem_limit_bytes=16 * 2**20),
    )(output, grad_images, grads, small, late)
    return (results[0][None], results[1][None], *results[2:])


def solution(mesh):
    in_specs = (
        P("fsdp", "tensor", None),
        P("fsdp", "tensor", None),
        P("fsdp"),
        P("fsdp"),
        P(None, None, "fsdp", "tensor"),
        P(),
        P(None, "tensor", "fsdp"),
        P(),
        P(),
        P(),
        P(),
        P(),
        P(None, "fsdp", "tensor"),
        P(),
        P(None, "tensor", "fsdp"),
        P(),
    )
    out_specs = (
        P("fsdp", "tensor", None),
        P("fsdp", "tensor", None),
        P(None, None, "fsdp", "tensor"),
        P(),
        P(None, "tensor", "fsdp"),
        P(),
        P(),
        P(),
        P(),
        P(),
        P(None, "fsdp", "tensor"),
        P(),
        P(None, "tensor", "fsdp"),
        P(),
    )
    body = fused_local if mesh.shape["fsdp"] == 16 else local
    return jax.shard_map(body, mesh=mesh, in_specs=in_specs, out_specs=out_specs, check_vma=False)
```
